32 devices in a mesh: tm: 4 (over y, x), lib: 8 (over z, core).
Axes of the slice: x: 2, y: 2, z: 4, core: 2. Of those that a mesh axis runs over, the one named last changes fastest.
Arguments:
- record: bfloat16 [24, 2048], P(None, 'tm'), may hold values from -6 to 6
- templates: bfloat16 [8, 4, 4, 24, 64, 256], P('lib', 'tm'), may hold values from -6 to 6
- owner: int32 [8, 2], P('lib'), may hold values from 0 to 3
- slot: int32 [8, 2], P('lib'), may hold values from 0 to 3
- mask: int32 [24], replicated, may hold values 0 or 1
Outputs:
- stacks: bfloat16 [8, 2, 64, 2048], P('lib', None, None, 'tm')
- best: float32 [2048], P('tm')
The draws below stay inside these ranges and needn't reach their ends.
Inputs may be any that keep to these rules, and one draw needn't show every extreme that they name: owner names a tm index. slot names a held block.
All inputs are finite; a program needn't handle non-finite values.
Results may differ from the reference program's by a relative error of at most 0.005.
Values may be sent and summed in bfloat16 or wider, within the bound.
No kernel may reach another device: no remote copies, remote signals or barrier semaphores. Data moves between devices by JAX's collectives and lax.ppermute only.
A program may use at most 64 MiB of HBM per device.

```python
import jax
import jax.numpy as jnp
from jax import lax

C = 24
L = 256
BLOCK = 64
SLOTS = 4
ROUNDS = 2
TIME = 2048
N_TM = 4
N_LIB = 8


def place_ends(values, rng, smallest, high):
    spot = [jax.random.randint(jax.random.fold_in(rng, axis), (), 0, length) for axis, length in enumerate(values.shape)]
    main_axis = values.shape.index(max(values.shape))
    neighbour = spot[:main_axis] + [(spot[main_axis] + 1) % values.shape[main_axis]] + spot[main_axis + 1:]
    return values.at[tuple(spot)].set(smallest).at[tuple(neighbour)].set(high)


def block_levels(stream_key, shape, split, least, largest):
    def one(axis_at, parts):
        heights = jax.random.uniform(jax.random.fold_in(jax.random.fold_in(stream_key, 6), axis_at), (parts,), jnp.float32, least / len(split), largest / len(split))
        return jnp.repeat(jnp.exp(heights), shape[axis_at] // parts).reshape((-1,) + (1,) * (len(shape) - axis_at - 1))

    level = one(*split[0])
    for cut in split[1:]:
        level = level * one(*cut)
    return level


def scatter_about(key, shape, scale, reach, shards=(), kind=jnp.bfloat16):
    entries = jax.random.normal(key, shape, jnp.float32) * scale
    if len(shards) > 0:
        entries = block_levels(key, shape, shards, -0.22, 0.18) * entries
    return jnp.clip(entries, min=-reach, max=reach).astype(kind)


def setup_inputs(seed: int = 0) -> dict:
    splits = jax.random.split(jax.random.key(seed), 6)
    return {
        "record": scatter_about(splits[0], (C, TIME), 1.0, 6.0, ((1, 4),)),
        "templates": scatter_about(splits[1], (N_LIB, N_TM, SLOTS, C, BLOCK, L), 1.0, 6.0, ((0, 8), (1, 4))),
        "owner": place_ends(jax.random.randint(splits[2], (N_LIB, ROUNDS), 0, N_TM), jax.random.fold_in(splits[2], 1), 0, N_TM - 1).astype(jnp.int32),
        "slot": place_ends(jax.random.randint(splits[3], (N_LIB, ROUNDS), 0, SLOTS), jax.random.fold_in(splits[3], 1), 0, SLOTS - 1).astype(jnp.int32),
        "mask": place_ends((jax.random.randint(splits[4], (C,), 0, 4) < 3).astype(jnp.int32), jax.random.fold_in(splits[4], 1), 0, 1),
    }


def grouped_corr(signal, kernel, groups, precision):
    return lax.conv_general_dilated(signal[None], kernel, (1,), 'VALID', dimension_numbers=('NCH', 'OIH', 'NCH'), feature_group_count=groups, precision=precision, preferred_element_type=jnp.float32)[0]

def reference(record, templates, owner, slot, mask):
    padded = jnp.concatenate([record, jnp.zeros((C, L), record.dtype)], axis=1)
    squares = padded.astype(jnp.float32) ** 2
    ones_kernel = jnp.ones((C, 1, L), jnp.float32)
    energy = grouped_corr(squares, ones_kernel, C, lax.Precision.HIGHEST)[:, :TIME]
    weight = mask.astype(jnp.float32)[:, None] / jnp.sqrt(jnp.maximum(energy, jnp.float32(L / 4)))
    count = jnp.maximum(jnp.sum(mask.astype(jnp.float32)), 1.0)
    gain = jnp.sqrt(jnp.float32(L)) / jnp.sqrt(count)

    def one_block(index):
        row = index // ROUNDS
        turn = index % ROUNDS
        holder = owner[row, turn]
        place = slot[row, turn]
        chosen = templates[row][holder][place]
        wide = chosen.astype(jnp.float32)
        norms = jnp.sqrt(lax.optimization_barrier(jnp.sum(wide * wide, axis=-1, keepdims=True)) + 1e-06)
        unit = (wide / norms).astype(jnp.bfloat16)
        kernel = unit.reshape(C * BLOCK, 1, L)
        corr = grouped_corr(padded, kernel, C, None)[:, :TIME].reshape(C, BLOCK, TIME)
        stack_f = lax.optimization_barrier(jnp.sum(corr * weight[:, None, :], axis=0)) * gain
        return (stack_f.astype(jnp.bfloat16), lax.optimization_barrier(jnp.max(stack_f, axis=0)))
    stacked, peaks = lax.map(one_block, jnp.arange(N_LIB * ROUNDS, dtype=jnp.int32))
    stacks = stacked.reshape(N_LIB, ROUNDS, BLOCK, TIME)
    best = lax.optimization_barrier(jnp.max(peaks, axis=0))
    return (stacks, best)
```

```python
import functools

import jax
import jax.numpy as jnp
from jax import lax
from jax.experimental import pallas as pl
from jax.experimental.pallas import tpu as pltpu
from jax.sharding import PartitionSpec as P

F32 = jnp.float32
BF16 = jnp.bfloat16
VMEM = pltpu.VMEM
SMEM = pltpu.SMEM


def swap(x, axis, flip):
    count = lax.axis_size(axis)
    return lax.ppermute(x, axis, [(i, i ^ flip) for i in range(count)])


def owns_any(owner_ref, me, rounds):
    mine = owner_ref[0, 0] == me
    for turn in range(1, rounds):
        mine = jnp.logical_or(mine, owner_ref[0, turn] == me)
    return mine


def prepare(me_ref, owner_ref, slot_ref, templates_ref, units_ref, held, sems):
    rounds, channels, block, taps = held.shape

    @pl.when(owns_any(owner_ref, me_ref[0], rounds))
    def _():
        copies = [
            pltpu.make_async_copy(templates_ref.at[slot_ref[0, r]], held.at[r], sems.at[r])
            for r in range(rounds)
        ]
        for copy in copies:
            copy.start()
        row = lax.broadcasted_iota(jnp.int32, (taps, taps), 0)
        col = lax.broadcasted_iota(jnp.int32, (taps, taps), 1)
        mirror = jnp.where(row + col == taps - 1, 1.0, 0.0).astype(BF16)
        for r in range(rounds):
            copies[r].wait()
            for c in range(channels):
                chosen = held[r, c]
                wide = chosen.astype(F32)
                norm = jnp.sum(wide * wide, axis=-1, keepdims=True) + 1e-06
                turned = jnp.dot(chosen, mirror, preferred_element_type=F32)
                units_ref[c, r * block : (r + 1) * block, :] = (turned * lax.rsqrt(norm)).astype(BF16)


def correlate(me_ref, owner_ref, mask_ref, *refs):
    *part_refs, units_ref, out_ref, spans = refs
    shards = len(part_refs)
    channels, samples = part_refs[0].shape
    rows, taps = units_ref.shape[1:]
    rounds = owner_ref.shape[1]
    me = me_ref[0]

    @pl.when(owns_any(owner_ref, me, rounds))
    def _():
        for d in range(shards):
            spans[me ^ d] = part_refs[d][...]
        spans[shards] = jnp.zeros((channels, samples), BF16)
        count = mask_ref[0]
        for c in range(1, channels):
            count = count + mask_ref[c]
        alive = jnp.maximum(jnp.full((8, 128), count, jnp.int32).astype(F32), 1.0)
        gain = (jnp.sqrt(F32(taps)) * lax.rsqrt(alive))[:1, :1]

        def shard(d, carry):
            j = me ^ d
            span = jnp.concatenate([spans[j], spans[j + 1][:, :taps]], axis=1)
            width = samples + taps
            wide = span.astype(F32)
            energy = wide * wide
            reach = 1
            while reach < taps:
                energy = energy + pltpu.roll(energy, width - reach, 1)
                reach *= 2
            weight = gain * lax.rsqrt(jnp.maximum(energy[:, :samples], F32(taps / 4)))
            total = jnp.zeros((rows, samples), F32)
            for c in range(channels):
                line = jnp.broadcast_to(span[c : c + 1, :], (taps // 2, width))
                slid = pltpu.roll(line, width - (taps // 2 - 1), 1, stride=1, stride_axis=0)
                window = jnp.concatenate(
                    [slid[:, taps // 2 : taps // 2 + samples], slid[:, :samples]], axis=0
                )
                corr = jnp.dot(units_ref[c], window, preferred_element_type=F32)
                total = total + corr * (weight[c : c + 1, :] * mask_ref[c].astype(F32))
            out_ref[d] = total.astype(BF16)
            return carry

        lax.fori_loop(0, shards, shard, 0)


def combine(me_ref, owner_ref, *refs):
    *held_refs, out_ref, best_ref = refs
    rounds, block, samples = out_ref.shape
    for r in range(rounds):
        source = owner_ref[0, r] ^ me_ref[0]
        for d, ref in enumerate(held_refs):

            @pl.when(source == d)
            def _():
                out_ref[r] = ref[r * block : (r + 1) * block, :]

    best_ref[...] = jnp.max(
        out_ref[...].astype(F32).reshape(rounds * block, samples), axis=0, keepdims=True
    )


def spec(space):
    return pl.BlockSpec(memory_space=space)


def on_device(record, templates, owner, slot, mask):
    channels, samples = record.shape
    slots, _, block, taps = templates.shape[2:]
    rounds = owner.shape[1]
    shards = lax.axis_size("tm")
    rows = rounds * block
    me = lax.axis_index("tm").astype(jnp.int32).reshape(1)

    parts = [record] + [swap(record, "tm", d) for d in range(1, shards)]

    units = pl.pallas_call(
        prepare,
        out_shape=jax.ShapeDtypeStruct((channels, rows, taps), BF16),
        in_specs=[spec(SMEM)] * 3 + [spec(pl.ANY)],
        out_specs=spec(VMEM),
        scratch_shapes=[
            VMEM((rounds, channels, block, taps), BF16),
            pltpu.SemaphoreType.DMA((rounds,)),
        ],
        compiler_params=pltpu.CompilerParams(vmem_limit_bytes=16 << 20),
        cost_estimate=pl.CostEstimate(flops=4 * 10**8, bytes_accessed=3 << 20, transcendentals=0),
        name="prepare",
    )(me, owner, slot, templates[0, 0])

    stacked = pl.pallas_call(
        correlate,
        out_shape=jax.ShapeDtypeStruct((shards, rows, samples), BF16),
        in_specs=[spec(SMEM)] * 3 + [spec(VMEM)] * (shards + 1),
        out_specs=spec(VMEM),
        scratch_shapes=[VMEM((shards + 1, channels, samples), BF16)],
        compiler_params=pltpu.CompilerParams(vmem_limit_bytes=24 << 20),
        name="correlate",
    )(me, owner, mask, *parts, units)

    held = [stacked[0]] + [swap(stacked[d], "tm", d) for d in range(1, shards)]

    stacks, best = pl.pallas_call(
        combine,
        out_shape=(
            jax.ShapeDtypeStruct((rounds, block, samples), BF16),
            jax.ShapeDtypeStruct((1, samples), F32),
        ),
        in_specs=[spec(SMEM)] * 2 + [spec(VMEM)] * shards,
        out_specs=(spec(VMEM), spec(VMEM)),
        compiler_params=pltpu.CompilerParams(vmem_limit_bytes=16 << 20),
        name="combine",
    )(me, owner, *held)

    rows_count = lax.axis_size("lib")
    step = 1
    while step < rows_count:
        flips = [step] if step == 1 or 2 * step >= rows_count else [step, 2 * step, 3 * step]
        others = [swap(best, "lib", flip) for flip in flips]
        best = functools.reduce(jnp.maximum, others, best)
        step *= 1 + len(flips)
    return stacks[None], best[0]


def solution(mesh):
    placed = (
        P(None, "tm"),
        P("lib", "tm", None, None, None, None),
        P("lib", None),
        P("lib", None),
        P(),
    )
    return jax.shard_map(
        on_device,
        mesh=mesh,
        in_specs=placed,
        out_specs=(P("lib", None, None, "tm"), P("tm")),
        check_vma=False,
    )
```

```python
import functools

import jax
import jax.numpy as jnp
from jax import lax
from jax.experimental import pallas as pl
from jax.experimental.pallas import tpu as pltpu
from jax.sharding import PartitionSpec as P

F32 = jnp.float32
BF16 = jnp.bfloat16
VMEM = pltpu.VMEM
SMEM = pltpu.SMEM
HBM = pltpu.HBM
CHUNKS = 2
TAIL = 16
PREPARE_VMEM = 51 << 20


def swap(x, axis, flip):
    count = lax.axis_size(axis)
    return lax.ppermute(x, axis, [(i, i ^ flip) for i in range(count)])


def pick(row, at):
    lane = lax.broadcasted_iota(jnp.int32, row.shape, 1)
    return jnp.sum(jnp.where(lane == at, row, 0))


def owned(owner_ref):
    return (owner_ref[...] == lax.axis_index("tm")).astype(jnp.int32)


def prepare(slot_ref, templates_ref, units_ref, held, sems):
    rounds, channels, block, taps = held.shape
    half = taps // 2
    chunks = sems.shape[1]
    step = channels // chunks

    slots = [pick(slot_ref[...], r) for r in range(rounds)]

    def fetch(r, k):
        part = pl.ds(k * step, step)
        return pltpu.make_async_copy(
            templates_ref.at[slots[r], part], held.at[r, part], sems.at[r, k]
        )

    for k in range(chunks):
        for r in range(rounds):
            fetch(r, k).start()
    row = lax.broadcasted_iota(jnp.int32, (half, half), 0)
    col = lax.broadcasted_iota(jnp.int32, (half, half), 1)
    mirror = jnp.where(row + col == half - 1, 1.0, 0.0).astype(BF16)
    for k in range(chunks):
        for r in range(rounds):
            fetch(r, k).wait()
        for c in range(k * step, (k + 1) * step):
            halves = [held[r, c, :, at : at + half] for r in range(rounds) for at in (0, half)]
            turned = jnp.dot(
                jnp.concatenate(halves, axis=0), mirror, preferred_element_type=F32
            )
            for r in range(rounds):
                wide = held[r, c].astype(F32)
                scale = lax.rsqrt(jnp.sum(wide * wide, axis=-1, keepdims=True) + 1e-06)
                for i, at in enumerate((0, half)):
                    first = (2 * r + i) * block
                    units_ref[c, r * block : (r + 1) * block, at : at + half] = (
                        turned[first : first + block] * scale
                    ).astype(BF16)


def correlate(flip, shards, ride, owner_ref, mask_ref, *refs):
    part_refs, refs = refs[:shards], refs[shards:]
    units_ref, out_ref, *refs = refs
    peak_ref = None if ride else refs.pop(0)
    spans, lines, weights = refs
    channels, samples = part_refs[0].shape
    rows, taps = units_ref.shape[1:]
    rounds = owner_ref.shape[1]
    half = taps // 2
    width = samples + taps
    lanes = 128
    me = lax.axis_index("tm")
    held = owned(owner_ref)
    mine = jnp.max(held) > 0

    def report(peak):
        if ride:
            out_ref[rows:] = jnp.broadcast_to(peak, (TAIL, samples)).astype(BF16)
        else:
            peak_ref[...] = peak

    @pl.when(jnp.logical_not(mine))
    def _():
        report(jnp.full((1, samples), -jnp.inf, F32))

    @pl.when(mine)
    def _():
        spans[shards] = jnp.zeros((channels, samples), BF16)
        for d in range(shards):
            spans[me ^ d] = part_refs[d][...]
        row = lax.broadcasted_iota(jnp.int32, (channels, channels), 0)
        col = lax.broadcasted_iota(jnp.int32, (channels, channels), 1)
        live = jnp.where(row == col, jnp.broadcast_to(mask_ref[...], row.shape), 0)
        live = jnp.sum(live, axis=1, keepdims=True).astype(F32)
        alive = jnp.maximum(jnp.sum(live, axis=0, keepdims=True), 1.0)
        gain = jnp.sqrt(F32(taps)) * lax.rsqrt(alive) * live
        lane = lax.broadcasted_iota(jnp.int32, (8, lanes), 1)
        behind = lane + lax.broadcasted_iota(jnp.int32, (8, lanes), 0)

        def build(c):
            line = lines[c]
            groups = []
            for g in range(half // 8):
                shift = half - 1 - 8 * g
                tiles = []
                for q in range(0, samples + half, lanes):
                    near, far = line[:, q : q + lanes], line[:, q + lanes : q + 2 * lanes]
                    mixed = jnp.where(behind >= shift, near, far)
                    tiles.append(pltpu.roll(mixed, lanes - shift, 1, stride=1, stride_axis=0))
                groups.append(jnp.concatenate(tiles, axis=1))
            return jnp.concatenate(groups, axis=0).astype(BF16)

        j = me ^ flip
        wide = jnp.concatenate([spans[j], spans[j + 1][:, :taps]], axis=1).astype(F32)
        energy = wide * wide
        reach = 1
        while reach < taps:
            energy = energy + pltpu.roll(energy, width - reach, 1)
            reach *= 2
        weight = gain * lax.rsqrt(jnp.maximum(energy[:, :samples], F32(taps / 4)))
        for c in range(channels):
            lines[c] = jnp.broadcast_to(wide[c : c + 1], (8, width))
            weights[c] = jnp.broadcast_to(weight[c : c + 1], (8, samples))
        stack = jnp.zeros((rows // 8, 8, samples), F32)
        for c in range(channels):
            window = build(c)
            corr = jnp.dot(
                units_ref[c],
                jnp.concatenate([window[:, :samples], window[:, half : half + samples]], axis=0),
                preferred_element_type=F32,
            )
            stack = stack + corr.reshape(rows // 8, 8, samples) * weights[c]
        out_ref[:rows] = stack.reshape(rows, samples).astype(BF16)
        peak = jnp.full((8, samples), -jnp.inf, F32)
        tall = rows // rounds // 8
        for r in range(rounds):
            top = jnp.max(stack[r * tall : (r + 1) * tall], axis=0)
            peak = jnp.where(held[:, r : r + 1] > 0, jnp.maximum(peak, top), peak)
        report(jnp.max(peak, axis=0, keepdims=True))


def combine(owner_ref, *refs):
    *held_refs, out_ref = refs
    rounds, block, samples = out_ref.shape
    for r in range(rounds):
        source = pick(owner_ref[...], r) ^ lax.axis_index("tm")
        for d, ref in enumerate(held_refs):

            @pl.when(source == d)
            def _():
                out_ref[r] = ref[r * block : (r + 1) * block, :]


def spec(space):
    return pl.BlockSpec(memory_space=space)


def on_device(record, templates, owner, slot, mask):
    channels, samples = record.shape
    slots, _, block, taps = templates.shape[2:]
    rounds = owner.shape[1]
    shards = lax.axis_size("tm")
    rows = rounds * block
    parts = [record] + [swap(record, "tm", d) for d in range(1, shards)]

    units = pl.pallas_call(
        prepare,
        out_shape=jax.ShapeDtypeStruct((channels, rows, taps), BF16),
        in_specs=[spec(VMEM), spec(HBM)],
        out_specs=spec(VMEM),
        scratch_shapes=[
            VMEM((rounds, channels, block, taps), BF16),
            pltpu.SemaphoreType.DMA((rounds, CHUNKS)),
        ],
        compiler_params=pltpu.CompilerParams(vmem_limit_bytes=PREPARE_VMEM),
        cost_estimate=pl.CostEstimate(flops=4 * 10**8, bytes_accessed=3 << 20, transcendentals=0),
        name="prepare",
    )(slot, templates[0, 0])

    def stack_at(flip, units, ride):
        stack = jax.ShapeDtypeStruct((rows + TAIL if ride else rows, samples), BF16)
        peak = jax.ShapeDtypeStruct((1, samples), F32)
        return pl.pallas_call(
            functools.partial(correlate, flip, shards, ride),
            out_shape=(stack,) if ride else (stack, peak),
            in_specs=[spec(VMEM)] * (shards + 3),
            out_specs=(spec(VMEM),) if ride else (spec(VMEM), spec(VMEM)),
            scratch_shapes=[
                VMEM((shards + 1, channels, samples), BF16),
                VMEM((channels, 8, samples + taps), F32),
                VMEM((channels, 8, samples), F32),
            ],
            compiler_params=pltpu.CompilerParams(vmem_limit_bytes=24 << 20),
            cost_estimate=pl.CostEstimate(
                flops=2 * rows * samples * channels * taps,
                bytes_accessed=4 << 20,
                transcendentals=0,
            ),
            name="correlate",
        )(owner, mask[None], *parts, units)

    held = {}
    for d in range(shards - 1, 1, -1):
        (piece,) = stack_at(d, units, True)
        held[d] = swap(piece, "tm", d)
        last = piece
    units, _ = lax.optimization_barrier((units, last))
    near, peak = stack_at(1, units, False)
    units, peak = lax.optimization_barrier((units, peak))
    near_peak = swap(peak, "tm", 1)
    held[0], best = stack_at(0, units, False)
    near, best = lax.optimization_barrier((near, best))
    held[1] = swap(near, "tm", 1)
    best = jnp.maximum(best, near_peak)
    for d in range(2, shards):
        best = jnp.maximum(best, held[d][rows : rows + 1].astype(F32))

    stacks = pl.pallas_call(
        combine,
        out_shape=jax.ShapeDtypeStruct((rounds, block, samples), BF16),
        in_specs=[spec(VMEM)] * (shards + 1),
        out_specs=spec(VMEM),
        compiler_params=pltpu.CompilerParams(vmem_limit_bytes=16 << 20),
        name="combine",
    )(owner, *[held[d] for d in range(shards)])

    rows_count = lax.axis_size("lib")
    step = 1
    while step < rows_count:
        flips = [step] if step == 1 or 2 * step >= rows_count else [step, 2 * step, 3 * step]
        others = [swap(best, "lib", flip) for flip in flips]
        best = functools.reduce(jnp.maximum, others, best)
        step *= 1 + len(flips)
    return stacks[None], best[0]


def solution(mesh):
    placed = (
        P(None, "tm"),
        P("lib", "tm", None, None, None, None),
        P("lib", None),
        P("lib", None),
        P(),
    )
    return jax.shard_map(
        on_device,
        mesh=mesh,
        in_specs=placed,
        out_specs=(P("lib", None, None, "tm"), P("tm")),
        check_vma=False,
    )
```

```python
import functools

import jax
import jax.numpy as jnp
from jax import lax
from jax.experimental import pallas as pl
from jax.experimental.pallas import tpu as pltpu
from jax.sharding import PartitionSpec as P

F32 = jnp.float32
BF16 = jnp.bfloat16
VMEM = pltpu.VMEM
SMEM = pltpu.SMEM
HBM = pltpu.HBM
CHUNKS = 2
TAIL = 16
PREPARE_VMEM = 51 << 20


def swap(x, axis, flip):
    count = lax.axis_size(axis)
    return lax.ppermute(x, axis, [(i, i ^ flip) for i in range(count)])


def pick(row, at):
    lane = lax.broadcasted_iota(jnp.int32, row.shape, 1)
    return jnp.sum(jnp.where(lane == at, row, 0))


def owned(owner_ref):
    return (owner_ref[...] == lax.axis_index("tm")).astype(jnp.int32)


def prepare(slot_ref, templates_ref, units_ref, held, sems):
    rounds, channels, block, taps = held.shape
    half = taps // 2
    chunks = sems.shape[1]
    step = channels // chunks

    slots = [pick(slot_ref[...], r) for r in range(rounds)]

    def fetch(r, k):
        part = pl.ds(k * step, step)
        return pltpu.make_async_copy(
            templates_ref.at[slots[r], part], held.at[r, part], sems.at[r, k]
        )

    for k in range(chunks):
        for r in range(rounds):
            fetch(r, k).start()
    row = lax.broadcasted_iota(jnp.int32, (half, half), 0)
    col = lax.broadcasted_iota(jnp.int32, (half, half), 1)
    mirror = jnp.where(row + col == half - 1, 1.0, 0.0).astype(BF16)
    for k in range(chunks):
        for r in range(rounds):
            fetch(r, k).wait()
        for c in range(k * step, (k + 1) * step):
            halves = [held[r, c, :, at : at + half] for r in range(rounds) for at in (0, half)]
            turned = jnp.dot(
                jnp.concatenate(halves, axis=0), mirror, preferred_element_type=F32
            )
            for r in range(rounds):
                wide = held[r, c].astype(F32)
                scale = lax.rsqrt(jnp.sum(wide * wide, axis=-1, keepdims=True) + 1e-06)
                for i, at in enumerate((0, half)):
                    first = (2 * r + i) * block
                    units_ref[c, r * block : (r + 1) * block, at : at + half] = (
                        turned[first : first + block] * scale
                    ).astype(BF16)


def correlate(flip, near, shards, ride, owner_ref, mask_ref, *refs):
    part_refs, refs = refs[: len(near)], refs[len(near) :]
    units_ref, out_ref, *refs = refs
    peak_ref = None if ride else refs.pop(0)
    spans, lines, weights = refs
    channels, samples = part_refs[0].shape
    rows, taps = units_ref.shape[1:]
    rounds = owner_ref.shape[1]
    half = taps // 2
    width = samples + taps
    lanes = 128
    me = lax.axis_index("tm")
    held = owned(owner_ref)
    mine = jnp.max(held) > 0

    def report(peak):
        if ride:
            out_ref[rows:] = jnp.broadcast_to(peak, (TAIL, samples)).astype(BF16)
        else:
            peak_ref[...] = peak

    @pl.when(jnp.logical_not(mine))
    def _():
        report(jnp.full((1, samples), -jnp.inf, F32))

    @pl.when(mine)
    def _():
        spans[shards] = jnp.zeros((channels, samples), BF16)
        for d, part_ref in zip(near, part_refs):
            spans[me ^ d] = part_ref[...]
        row = lax.broadcasted_iota(jnp.int32, (channels, channels), 0)
        col = lax.broadcasted_iota(jnp.int32, (channels, channels), 1)
        live = jnp.where(row == col, jnp.broadcast_to(mask_ref[...], row.shape), 0)
        live = jnp.sum(live, axis=1, keepdims=True).astype(F32)
        alive = jnp.maximum(jnp.sum(live, axis=0, keepdims=True), 1.0)
        gain = jnp.sqrt(F32(taps)) * lax.rsqrt(alive) * live
        lane = lax.broadcasted_iota(jnp.int32, (8, lanes), 1)
        behind = lane + lax.broadcasted_iota(jnp.int32, (8, lanes), 0)

        def build(c):
            line = lines[c]
            groups = []
            for g in range(half // 8):
                shift = half - 1 - 8 * g
                tiles = []
                for q in range(0, samples + half, lanes):
                    near, far = line[:, q : q + lanes], line[:, q + lanes : q + 2 * lanes]
                    mixed = jnp.where(behind >= shift, near, far)
                    tiles.append(pltpu.roll(mixed, lanes - shift, 1, stride=1, stride_axis=0))
                groups.append(jnp.concatenate(tiles, axis=1))
            return jnp.concatenate(groups, axis=0).astype(BF16)

        j = me ^ flip
        wide = jnp.concatenate([spans[j], spans[j + 1][:, :taps]], axis=1).astype(F32)
        energy = wide * wide
        reach = 1
        while reach < taps:
            energy = energy + pltpu.roll(energy, width - reach, 1)
            reach *= 2
        weight = gain * lax.rsqrt(jnp.maximum(energy[:, :samples], F32(taps / 4)))
        for c in range(channels):
            lines[c] = jnp.broadcast_to(wide[c : c + 1], (8, width))
            weights[c] = jnp.broadcast_to(weight[c : c + 1], (8, samples))
        stack = jnp.zeros((rows // 8, 8, samples), F32)
        for c in range(channels):
            window = build(c)
            corr = jnp.dot(
                units_ref[c],
                jnp.concatenate([window[:, :samples], window[:, half : half + samples]], axis=0),
                preferred_element_type=F32,
            )
            stack = stack + corr.reshape(rows // 8, 8, samples) * weights[c]
        out_ref[:rows] = stack.reshape(rows, samples).astype(BF16)
        peak = jnp.full((8, samples), -jnp.inf, F32)
        tall = rows // rounds // 8
        for r in range(rounds):
            top = jnp.max(stack[r * tall : (r + 1) * tall], axis=0)
            peak = jnp.where(held[:, r : r + 1] > 0, jnp.maximum(peak, top), peak)
        report(jnp.max(peak, axis=0, keepdims=True))


def combine(owner_ref, *refs):
    *held_refs, out_ref = refs
    rounds, block, samples = out_ref.shape
    for r in range(rounds):
        source = pick(owner_ref[...], r) ^ lax.axis_index("tm")
        for d, ref in enumerate(held_refs):

            @pl.when(source == d)
            def _():
                out_ref[r] = ref[r * block : (r + 1) * block, :]


def spec(space):
    return pl.BlockSpec(memory_space=space)


def on_device(record, templates, owner, slot, mask):
    channels, samples = record.shape
    slots, _, block, taps = templates.shape[2:]
    rounds = owner.shape[1]
    shards = lax.axis_size("tm")
    rows = rounds * block
    parts = [record] + [swap(record, "tm", d) for d in range(1, shards)]

    units = pl.pallas_call(
        prepare,
        out_shape=jax.ShapeDtypeStruct((channels, rows, taps), BF16),
        in_specs=[spec(VMEM), spec(HBM)],
        out_specs=spec(VMEM),
        scratch_shapes=[
            VMEM((rounds, channels, block, taps), BF16),
            pltpu.SemaphoreType.DMA((rounds, CHUNKS)),
        ],
        compiler_params=pltpu.CompilerParams(vmem_limit_bytes=PREPARE_VMEM),
        cost_estimate=pl.CostEstimate(flops=4 * 10**8, bytes_accessed=3 << 20, transcendentals=0),
        name="prepare",
    )(slot, templates[0, 0])

    def stack_at(flip, units, ride):
        near = [flip]
        while len(near) <= (shards - 1).bit_length():
            near.append(flip ^ ((1 << len(near)) - 1))
        stack = jax.ShapeDtypeStruct((rows + TAIL if ride else rows, samples), BF16)
        peak = jax.ShapeDtypeStruct((1, samples), F32)
        return pl.pallas_call(
            functools.partial(correlate, flip, near, shards, ride),
            out_shape=(stack,) if ride else (stack, peak),
            in_specs=[spec(VMEM)] * (len(near) + 3),
            out_specs=(spec(VMEM),) if ride else (spec(VMEM), spec(VMEM)),
            scratch_shapes=[
                VMEM((shards + 1, channels, samples), BF16),
                VMEM((channels, 8, samples + taps), F32),
                VMEM((channels, 8, samples), F32),
            ],
            compiler_params=pltpu.CompilerParams(vmem_limit_bytes=24 << 20),
            cost_estimate=pl.CostEstimate(
                flops=2 * rows * samples * channels * taps,
                bytes_accessed=4 << 20,
                transcendentals=0,
            ),
            name="correlate",
        )(owner, mask[None], *[parts[d] for d in near], units)

    *early, late = [1, 3, *range(4, shards), 2]
    held = {}
    for d in early:
        (last,) = stack_at(d, units, True)
        held[d] = swap(last, "tm", d)
    units, _ = lax.optimization_barrier((units, last))
    near, peak = stack_at(late, units, False)
    units, peak = lax.optimization_barrier((units, peak))
    near_peak = swap(peak, "tm", late)
    held[0], best = stack_at(0, units, False)
    near, best = lax.optimization_barrier((near, best))
    held[late] = swap(near, "tm", late)
    best = jnp.maximum(best, near_peak)
    for d in early:
        best = jnp.maximum(best, held[d][rows : rows + 1].astype(F32))

    stacks = pl.pallas_call(
        combine,
        out_shape=jax.ShapeDtypeStruct((rounds, block, samples), BF16),
        in_specs=[spec(VMEM)] * (shards + 1),
        out_specs=spec(VMEM),
        compiler_params=pltpu.CompilerParams(vmem_limit_bytes=16 << 20),
        name="combine",
    )(owner, *[held[d] for d in range(shards)])

    rows_count = lax.axis_size("lib")
    step = 1
    while step < rows_count:
        flips = [step] if step == 1 or 2 * step >= rows_count else [step, 2 * step, 3 * step]
        others = [swap(best, "lib", flip) for flip in flips]
        best = functools.reduce(jnp.maximum, others, best)
        step *= 1 + len(flips)
    return stacks[None], best[0]


def solution(mesh):
    placed = (
        P(None, "tm"),
        P("lib", "tm", None, None, None, None),
        P("lib", None),
        P("lib", None),
        P(),
    )
    return jax.shard_map(
        on_device,
        mesh=mesh,
        in_specs=placed,
        out_specs=(P("lib", None, None, "tm"), P("tm")),
        check_vma=False,
    )
```

```python
import functools

import jax
import jax.numpy as jnp
from jax import lax
from jax.experimental import pallas as pl
from jax.experimental.pallas import tpu as pltpu
from jax.sharding import PartitionSpec as P

F32 = jnp.float32
BF16 = jnp.bfloat16
VMEM = pltpu.VMEM
SMEM = pltpu.SMEM
HBM = pltpu.HBM
CHUNKS = 2
TAIL = 16
PREPARE_VMEM = 51 << 20


def swap(x, axis, flip):
    count = lax.axis_size(axis)
    return lax.ppermute(x, axis, [(i, i ^ flip) for i in range(count)])


def pick(row, at):
    lane = lax.broadcasted_iota(jnp.int32, row.shape, 1)
    return jnp.sum(jnp.where(lane == at, row, 0))


def owned(owner_ref):
    return (owner_ref[...] == lax.axis_index("tm")).astype(jnp.int32)


def prepare(slot_ref, templates_ref, units_ref, held, sems):
    rounds, channels, block, taps = held.shape
    half = taps // 2
    chunks = sems.shape[1]
    step = channels // chunks

    slots = [pick(slot_ref[...], r) for r in range(rounds)]

    def fetch(r, k):
        part = pl.ds(k * step, step)
        return pltpu.make_async_copy(
            templates_ref.at[slots[r], part], held.at[r, part], sems.at[r, k]
        )

    for k in range(chunks):
        for r in range(rounds):
            fetch(r, k).start()
    row = lax.broadcasted_iota(jnp.int32, (half, half), 0)
    col = lax.broadcasted_iota(jnp.int32, (half, half), 1)
    mirror = jnp.where(row + col == half - 1, 1.0, 0.0).astype(BF16)
    for k in range(chunks):
        for r in range(rounds):
            fetch(r, k).wait()
        for c in range(k * step, (k + 1) * step):
            halves = [held[r, c, :, at : at + half] for r in range(rounds) for at in (0, half)]
            turned = jnp.dot(
                jnp.concatenate(halves, axis=0), mirror, preferred_element_type=F32
            )
            for r in range(rounds):
                wide = held[r, c].astype(F32)
                scale = lax.rsqrt(jnp.sum(wide * wide, axis=-1, keepdims=True) + 1e-06)
                for i, at in enumerate((0, half)):
                    first = (2 * r + i) * block
                    units_ref[c, r * block : (r + 1) * block, at : at + half] = (
                        turned[first : first + block] * scale
                    ).astype(BF16)


def correlate(flip, near, shards, ride, owner_ref, mask_ref, *refs):
    part_refs, refs = refs[: len(near)], refs[len(near) :]
    units_ref, out_ref, *refs = refs
    peak_ref = None if ride else refs.pop(0)
    spans, lines, weights = refs
    channels, samples = part_refs[0].shape
    rows, taps = units_ref.shape[1:]
    rounds = owner_ref.shape[1]
    half = taps // 2
    width = samples + taps
    lanes = 128
    me = lax.axis_index("tm")
    held = owned(owner_ref)
    mine = jnp.max(held) > 0

    def report(peak):
        if ride:
            out_ref[rows:] = jnp.broadcast_to(peak, (TAIL, samples)).astype(BF16)
        else:
            peak_ref[...] = peak

    @pl.when(jnp.logical_not(mine))
    def _():
        report(jnp.full((1, samples), -jnp.inf, F32))

    @pl.when(mine)
    def _():
        spans[shards] = jnp.zeros((channels, samples), BF16)
        for d, part_ref in zip(near, part_refs):
            spans[me ^ d] = part_ref[...]
        row = lax.broadcasted_iota(jnp.int32, (channels, channels), 0)
        col = lax.broadcasted_iota(jnp.int32, (channels, channels), 1)
        live = jnp.where(row == col, jnp.broadcast_to(mask_ref[...], row.shape), 0)
        live = jnp.sum(live, axis=1, keepdims=True).astype(F32)
        alive = jnp.maximum(jnp.sum(live, axis=0, keepdims=True), 1.0)
        gain = jnp.sqrt(F32(taps)) * lax.rsqrt(alive) * live
        lane = lax.broadcasted_iota(jnp.int32, (8, lanes), 1)
        behind = lane + lax.broadcasted_iota(jnp.int32, (8, lanes), 0)

        def build(c):
            line = lines[c]
            groups = []
            for g in range(half // 8):
                shift = half - 1 - 8 * g
                tiles = []
                for q in range(0, samples + half, lanes):
                    near, far = line[:, q : q + lanes], line[:, q + lanes : q + 2 * lanes]
                    mixed = jnp.where(behind >= shift, near, far)
                    tiles.append(pltpu.roll(mixed, lanes - shift, 1, stride=1, stride_axis=0))
                groups.append(jnp.concatenate(tiles, axis=1))
            return jnp.concatenate(groups, axis=0).astype(BF16)

        j = me ^ flip
        wide = jnp.concatenate([spans[j], spans[j + 1][:, :taps]], axis=1).astype(F32)
        energy = wide * wide
        reach = 1
        while reach < taps:
            energy = energy + pltpu.roll(energy, width - reach, 1)
            reach *= 2
        weight = gain * lax.rsqrt(jnp.maximum(energy[:, :samples], F32(taps / 4)))
        for c in range(channels):
            lines[c] = jnp.broadcast_to(wide[c : c + 1], (8, width))
            weights[c] = jnp.broadcast_to(weight[c : c + 1], (8, samples))
        stack = jnp.zeros((rows // 8, 8, samples), F32)
        for c in range(channels):
            window = build(c)
            corr = jnp.dot(
                units_ref[c],
                jnp.concatenate([window[:, :samples], window[:, half : half + samples]], axis=0),
                preferred_element_type=F32,
            )
            stack = stack + corr.reshape(rows // 8, 8, samples) * weights[c]
        out_ref[:rows] = stack.reshape(rows, samples).astype(BF16)
        peak = jnp.full((8, samples), -jnp.inf, F32)
        tall = rows // rounds // 8
        for r in range(rounds):
            top = jnp.max(stack[r * tall : (r + 1) * tall], axis=0)
            peak = jnp.where(held[:, r : r + 1] > 0, jnp.maximum(peak, top), peak)
        report(jnp.max(peak, axis=0, keepdims=True))


def combine(owner_ref, *refs):
    *held_refs, out_ref = refs
    rounds, block, samples = out_ref.shape
    me = lax.axis_index("tm")
    for r in range(rounds):
        source = pick(owner_ref[...], r) ^ me
        taken = held_refs[0][r * block : (r + 1) * block, :]
        for d in range(1, len(held_refs)):
            taken = jnp.where(source == d, held_refs[d][r * block : (r + 1) * block, :], taken)
        out_ref[r] = taken


def spec(space):
    return pl.BlockSpec(memory_space=space)


def on_device(record, templates, owner, slot, mask):
    channels, samples = record.shape
    slots, _, block, taps = templates.shape[2:]
    rounds = owner.shape[1]
    shards = lax.axis_size("tm")
    rows = rounds * block
    parts = [record] + [swap(record, "tm", d) for d in range(1, shards)]

    units = pl.pallas_call(
        prepare,
        out_shape=jax.ShapeDtypeStruct((channels, rows, taps), BF16),
        in_specs=[spec(VMEM), spec(HBM)],
        out_specs=spec(VMEM),
        scratch_shapes=[
            VMEM((rounds, channels, block, taps), BF16),
            pltpu.SemaphoreType.DMA((rounds, CHUNKS)),
        ],
        compiler_params=pltpu.CompilerParams(vmem_limit_bytes=PREPARE_VMEM),
        cost_estimate=pl.CostEstimate(flops=4 * 10**8, bytes_accessed=3 << 20, transcendentals=0),
        name="prepare",
    )(slot, templates[0, 0])

    def stack_at(flip, units, ride):
        near = [flip]
        while len(near) <= (shards - 1).bit_length():
            near.append(flip ^ ((1 << len(near)) - 1))
        stack = jax.ShapeDtypeStruct((rows + TAIL if ride else rows, samples), BF16)
        peak = jax.ShapeDtypeStruct((1, samples), F32)
        return pl.pallas_call(
            functools.partial(correlate, flip, near, shards, ride),
            out_shape=(stack,) if ride else (stack, peak),
            in_specs=[spec(VMEM)] * (len(near) + 3),
            out_specs=(spec(VMEM),) if ride else (spec(VMEM), spec(VMEM)),
            scratch_shapes=[
                VMEM((shards + 1, channels, samples), BF16),
                VMEM((channels, 8, samples + taps), F32),
                VMEM((channels, 8, samples), F32),
            ],
            compiler_params=pltpu.CompilerParams(vmem_limit_bytes=24 << 20),
            cost_estimate=pl.CostEstimate(
                flops=2 * rows * samples * channels * taps,
                bytes_accessed=4 << 20,
                transcendentals=0,
            ),
            name="correlate",
        )(owner, mask[None], *[parts[d] for d in near], units)

    *early, late = [1, 3, *range(4, shards), 2]
    held = {}
    for d in early:
        (last,) = stack_at(d, units, True)
        held[d] = swap(last, "tm", d)
    units, _ = lax.optimization_barrier((units, last))
    near, peak = stack_at(late, units, False)
    units, peak = lax.optimization_barrier((units, peak))
    near_peak = swap(peak, "tm", late)
    held[0], best = stack_at(0, units, False)
    near, best = lax.optimization_barrier((near, best))
    held[late] = swap(near, "tm", late)
    best = jnp.maximum(best, near_peak)
    for d in early:
        best = jnp.maximum(best, held[d][rows : rows + 1].astype(F32))

    stacks = pl.pallas_call(
        combine,
        out_shape=jax.ShapeDtypeStruct((rounds, block, samples), BF16),
        in_specs=[spec(VMEM)] * (shards + 1),
        out_specs=spec(VMEM),
        compiler_params=pltpu.CompilerParams(vmem_limit_bytes=16 << 20),
        name="combine",
    )(owner, *[held[d] for d in range(shards)])

    rows_count = lax.axis_size("lib")
    step = 1
    while step < rows_count:
        flips = [step] if step == 1 or 2 * step >= rows_count else [step, 2 * step, 3 * step]
        others = [swap(best, "lib", flip) for flip in flips]
        best = functools.reduce(jnp.maximum, others, best)
        step *= 1 + len(flips)
    return stacks[None], best[0]


def solution(mesh):
    placed = (
        P(None, "tm"),
        P("lib", "tm", None, None, None, None),
        P("lib", None),
        P("lib", None),
        P(),
    )
    return jax.shard_map(
        on_device,
        mesh=mesh,
        in_specs=placed,
        out_specs=(P("lib", None, None, "tm"), P("tm")),
        check_vma=False,
    )
```
